512 devices in a mesh: blk: 32 (over x, z), order: 16 (over y, core).
Axes of the slice: x: 4, y: 8, z: 8, core: 2. Of those that a mesh axis runs over, the one named last changes fastest.
Arguments:
- cotangent: bfloat16 [8, 512, 4096], P(None, 'blk', 'order'), may hold values from -6 to 6
- cycle_slot: int32 [512], P('blk'), may hold values from 1 to 4095, as said below
- order_slot: int32 [1024], replicated, may hold values from 0 to 1023, each once
- legendre_healpix: bfloat16 [1024, 512, 1024], P('order', 'blk'), may hold values from -0.25 to 0.25
- legendre_gauss: bfloat16 [1024, 128, 1024], P('order', 'blk'), may hold values from -0.1875 to 0.1875
Outputs:
- gauss_cotangent: float32 [2048, 8, 128], P('order', None, 'blk')
The draws below stay inside these ranges and needn't reach their ends.
Inputs may be any that keep to these rules, and one draw needn't show every extreme that they name: `cycle_slot`: distinct HEALPix cycle numbers counted from the north pole; both polar end cycles are present. `order_slot`: each wavenumber once.
All inputs are finite; a program needn't handle non-finite values.
Results may differ from the reference program's by a relative error of at most 0.0023.
Values may be sent and summed in bfloat16 or wider, within the bound.
No kernel may reach another device: no remote copies, remote signals or barrier semaphores. Data moves between devices by JAX's collectives and lax.ppermute only.
A program may use at most 64 MiB of HBM per device.

```python
import math
import jax
import jax.numpy as jnp
from jax import lax

NSIDE = 1024
ORDERS = 1024
NPIX = 4096
NLON = 2048
FIELDS = 8
CYCLES = 512
GRINGS = 128


def draw_cycle_slot(key, part):
    key = jax.random.fold_in(key, 11)
    first_key, second_key = jax.random.split(key)
    inner = jax.random.permutation(first_key, 4 * NSIDE - 3)[:CYCLES - 2].astype(jnp.int32) + 2
    values = jnp.concatenate([jnp.asarray([1, 4 * NSIDE - 1], jnp.int32), inner])
    placing = jax.random.permutation(second_key, CYCLES)
    return values[placing].astype(jnp.int32)


def shard_levels(key, shape, cuts, least, high):
    loudness = 1.0
    for dim, parts in cuts:
        steps = jax.random.uniform(jax.random.fold_in(jax.random.fold_in(key, 6), dim), (parts,), jnp.float32, least / len(cuts), high / len(cuts))
        loudness = loudness * jnp.repeat(jnp.exp(steps), shape[dim] // parts).reshape((-1,) + (1,) * (len(shape) - 1 - dim))
    return loudness


def normal_values(own_key, shape, scale, reach, cuts=(), held_as=jnp.bfloat16):
    level = shard_levels(own_key, shape, cuts, -0.22, 0.18) if cuts else 1.0
    drawn = jax.random.normal(own_key, shape, jnp.float32) * scale * level
    return jnp.minimum(jnp.maximum(drawn, -reach), reach).astype(held_as)


def setup_inputs(seed: int = 0) -> dict:
    arg_keys = jax.random.split(jax.random.key(seed), 6)
    cotangent = normal_values(arg_keys[0], (FIELDS, CYCLES, NPIX), 1.0, 6.0, ((1, 32), (2, 16)))
    cycle_slot = draw_cycle_slot(jax.random.fold_in(arg_keys[5], 71), 0)
    order_slot = jax.random.permutation(arg_keys[2], ORDERS).astype(jnp.int32)
    legendre_healpix = normal_values(arg_keys[3], (ORDERS, CYCLES, ORDERS), CYCLES ** -0.5, 0.25, ((0, 16), (1, 32)))
    legendre_gauss = normal_values(arg_keys[4], (ORDERS, GRINGS, ORDERS), ORDERS ** -0.5, 0.1875, ((0, 16), (1, 32)))
    return dict(cotangent=cotangent, cycle_slot=cycle_slot, order_slot=order_slot, legendre_healpix=legendre_healpix, legendre_gauss=legendre_gauss)


def cycle_geometry(cycle_slot, nside, npix):
    cycle_number = cycle_slot.astype(jnp.int32)
    nearest = jnp.minimum(jnp.minimum(cycle_number, nside), 4 * nside - cycle_number)
    powers = jnp.asarray([2 ** power_index for power_index in range(nside.bit_length())], jnp.int32)
    rounded = lax.optimization_barrier(jnp.sum(jnp.where(powers[None, :] < nearest[:, None], powers[None, :], 0), axis=1)).astype(jnp.int32) + 1
    cycle_length = 4 * rounded
    stride = (npix // cycle_length).astype(jnp.int32)
    shifted = (nearest < nside) | ((cycle_number - nside) % 2 == 0)
    twice_offset = jnp.where(shifted, stride, 0).astype(jnp.int32)
    cycle_scale = 1.0 / jnp.sqrt(cycle_length.astype(jnp.float32))
    return (stride, twice_offset, cycle_scale)

def fourier_sums(data, columns, orders, npix):
    count = orders.shape[0]
    width = math.gcd(count, 128)
    blocks = orders.reshape(count // width, width)

    def one_block(block_orders):
        product = block_orders[:, None] * columns[None, :] % npix
        angle = product.astype(jnp.float32) * (2.0 * math.pi / npix)
        table = jnp.concatenate([jnp.cos(angle), jnp.sin(angle)], axis=0).astype(jnp.bfloat16)
        both = lax.dot_general(table, data, (((1,), (1,)), ((), ())), preferred_element_type=jnp.float32)
        return (both[:width], both[width:])
    cos_sums, sin_sums = lax.map(one_block, blocks)
    return (cos_sums.reshape(count, -1), sin_sums.reshape(count, -1))

def rotate(cos_sums, sin_sums, orders, twice_offset, cycle_scale, npix):
    product = orders[:, None] * twice_offset[None, :] % (2 * npix)
    phase = product.astype(jnp.float32) * (math.pi / npix)
    cos_phase = jnp.cos(phase)
    sin_phase = jnp.sin(phase)
    real_part = cycle_scale[None, :] * (cos_phase * cos_sums - sin_phase * sin_sums)
    imag_part = -cycle_scale[None, :] * (sin_phase * cos_sums + cos_phase * sin_sums)
    return jnp.stack([real_part, imag_part], axis=1)

def reference(cotangent, cycle_slot, order_slot, legendre_healpix, legendre_gauss):
    stride, twice_offset, cycle_scale = cycle_geometry(cycle_slot, NSIDE, NPIX)
    columns = jnp.arange(NPIX, dtype=jnp.int32)
    keep = (columns[None, :] % stride[:, None] == 0).astype(jnp.bfloat16)
    masked = (cotangent * keep[None]).reshape(FIELDS * CYCLES, NPIX)
    cos_sums, sin_sums = fourier_sums(masked, columns, order_slot.astype(jnp.int32), NPIX)
    fourier = rotate(cos_sums, sin_sums, order_slot.astype(jnp.int32), jnp.tile(twice_offset, FIELDS), jnp.tile(cycle_scale, FIELDS), NPIX)
    fourier = fourier.reshape(ORDERS, 2, FIELDS, CYCLES)
    block = math.gcd(ORDERS, 32)
    count = ORDERS // block
    degree_index = jnp.arange(ORDERS, dtype=jnp.int32)

    def per_block(items):
        healpix_rows, fourier_rows, gauss_rows, block_orders = items
        table_f = healpix_rows.astype(jnp.float32)
        data_f = fourier_rows.astype(jnp.float32)
        spectral = jnp.einsum('srl,scfr->slcf', table_f, data_f, precision=lax.Precision.HIGHEST)
        live = (degree_index[None, :] >= block_orders[:, None]).astype(jnp.float32)
        spectral = spectral * live[:, :, None, None]
        return jnp.einsum('sgl,slcf->scfg', gauss_rows.astype(jnp.float32), spectral, precision=lax.Precision.HIGHEST)
    gaussian = lax.map(per_block, (legendre_healpix.reshape(count, block, CYCLES, ORDERS), fourier.reshape(count, block, 2, FIELDS, CYCLES), legendre_gauss.reshape(count, block, GRINGS, ORDERS), order_slot.astype(jnp.int32).reshape(count, block)))
    flat = gaussian.reshape(ORDERS, 2, FIELDS * GRINGS)
    longitude = jnp.arange(NLON, dtype=jnp.int32)
    product = longitude[:, None] * order_slot.astype(jnp.int32)[None, :] % NLON
    angle = product.astype(jnp.float32) * (2.0 * math.pi / NLON)
    result = jnp.dot(jnp.cos(angle), flat[:, 0], precision=lax.Precision.HIGHEST) - jnp.dot(jnp.sin(angle), flat[:, 1], precision=lax.Precision.HIGHEST)
    result = result * (1.0 / math.sqrt(ORDERS))
    return result.reshape(NLON, FIELDS, GRINGS)
```

```python
import math

import jax
import jax.numpy as jnp
from jax import lax
from jax.experimental import pallas as pl
from jax.experimental.pallas import tpu as pltpu
from jax.sharding import PartitionSpec as P

NPIX, NLON, NSIDE = 4096, 2048, 1024
FIELDS, ORDERS, DEGREES = 8, 1024, 1024
N_ORDER, N_BLK = 16, 32
SLOTS = ORDERS // N_ORDER
NX, NZA, NZB = 4, 2, 4
NE = NX * NZA
SE = SLOTS // NE
NS = SE // NZB
RB = 16
GB = 4
GROUP_E = [[x * 8 + zb * 2 + za for x in range(NX) for za in range(NZA)] for zb in range(NZB)]
GROUP_Z = [[x * 8 + zb * 2 + za for zb in range(NZB)] for x in range(NX) for za in range(NZA)]
GROUP_ALL = [
    [x * 8 + zb * 2 + za for x in range(NX) for za in range(NZA) for zb in range(NZB)]
]
BF16, F32 = jnp.bfloat16, jnp.float32


def exchange(value, axis, groups=None):
    return lax.all_to_all(
        value, axis, split_axis=0, concat_axis=0, tiled=True, axis_index_groups=groups
    )


def split2(value):
    high = value.astype(BF16)
    return high, (value - high.astype(F32)).astype(BF16)


def params(mib):
    return pltpu.CompilerParams(vmem_limit_bytes=mib << 20)


def cycle_geometry(cycle_slot):
    nearest = jnp.minimum(jnp.minimum(cycle_slot, NSIDE), 4 * NSIDE - cycle_slot)
    powers = jnp.asarray([2**index for index in range(NSIDE.bit_length())], jnp.int32)
    rounded = jnp.sum(jnp.where(powers < nearest, powers, 0)) + 1
    cycle_length = 4 * rounded
    stride = NPIX // cycle_length
    shifted = (nearest < NSIDE) | ((cycle_slot - NSIDE) % 2 == 0)
    twice_offset = jnp.where(shifted, stride, 0)
    cycle_scale = 1.0 / jnp.sqrt(cycle_length.astype(F32))
    return stride, twice_offset, cycle_scale


def table_kernel(ca_ref, sa_ref, cb_ref, sb_ref, out_ref):
    for s in range(SE):
        lanes = slice(s * 128, s * 128 + 128)
        cb, sb = cb_ref[:, lanes], sb_ref[:, lanes]
        for a in range(4):
            ca, sa = ca_ref[0, a : a + 1, lanes], sa_ref[0, a : a + 1, lanes]
            rows = slice(a * 64, a * 64 + 64)
            out_ref[rows, s * 256 : s * 256 + 128] = (ca * cb - sa * sb).astype(BF16)
            out_ref[rows, s * 256 + 128 : s * 256 + 256] = (sa * cb + ca * sb).astype(BF16)


def pixel_table(orders):
    index = jnp.arange(64, dtype=jnp.int32)
    coarse = (index[:, None] * orders[None, :] % 64).astype(F32) * (2.0 * math.pi / 64)
    fine = (index[:, None] * orders[None, :] % NPIX).astype(F32) * (2.0 * math.pi / NPIX)
    ca, sa = jnp.cos(coarse).reshape(16, 4, ORDERS), jnp.sin(coarse).reshape(16, 4, ORDERS)
    part = pl.BlockSpec((1, 4, ORDERS), lambda i: (i, 0, 0))
    whole = pl.BlockSpec((64, ORDERS), lambda i: (0, 0))
    return pl.pallas_call(
        table_kernel,
        grid=(16,),
        out_shape=jax.ShapeDtypeStruct((NPIX, 2 * ORDERS), BF16),
        in_specs=[part, part, whole, whole],
        out_specs=pl.BlockSpec((256, 2 * ORDERS), lambda i: (i, 0)),
        compiler_params=params(32),
    )(ca, sa, jnp.cos(fine), jnp.sin(fine))


def pixel_kernel(stride_ref, x_ref, table_ref, rc_ref, rs_ref, out_ref, acc_ref):
    step = pl.program_id(0)
    column = step * 256 + lax.broadcasted_iota(jnp.int32, (FIELDS, 256), 1)
    keep = (column & (stride_ref[0] - 1)) == 0
    masked = jnp.where(keep, x_ref[0].astype(F32), 0.0).astype(BF16)
    part = jnp.dot(masked, table_ref[...], preferred_element_type=F32)

    @pl.when(step == 0)
    def _():
        acc_ref[...] = part

    @pl.when(step > 0)
    def _():
        acc_ref[...] += part

    @pl.when(step == 15)
    def _():
        rows = []
        for s in range(SE):
            csum = acc_ref[:, s * 256 : s * 256 + 128]
            ssum = acc_ref[:, s * 256 + 128 : s * 256 + 256]
            rc, rs = rc_ref[s : s + 1, :], rs_ref[s : s + 1, :]
            rows.append(rc * csum - rs * ssum)
            rows.append(-(rs * csum + rc * ssum))
        out_ref[...] = jnp.concatenate(rows, axis=0).T


def pixel_sums(stride, x, table, rc, rs):
    return pl.pallas_call(
        pixel_kernel,
        grid=(16,),
        out_shape=jax.ShapeDtypeStruct((128, 128), F32),
        in_specs=[
            pl.BlockSpec(memory_space=pltpu.SMEM),
            pl.BlockSpec((1, FIELDS, 256), lambda i: (i, 0, 0)),
            pl.BlockSpec((256, 2 * ORDERS), lambda i: (i, 0)),
            pl.BlockSpec((SE, 128), lambda i: (0, 0)),
            pl.BlockSpec((SE, 128), lambda i: (0, 0)),
        ],
        out_specs=pl.BlockSpec((128, 128), lambda i: (0, 0)),
        scratch_shapes=[pltpu.VMEM((FIELDS, 2 * ORDERS), F32)],
        compiler_params=params(32),
    )(stride, x, table, rc, rs)


def synthesis_kernel(order_ref, fourier_ref, legendre_ref, out_ref):
    high, low = split2(fourier_ref[...].T)
    degree = lax.broadcasted_iota(jnp.int32, (16, DEGREES), 1)
    for s in range(SE):
        rows = slice(s * 16, s * 16 + 16)
        left = jnp.concatenate([high[rows], low[rows]], axis=0)
        right = jnp.concatenate([legendre_ref[e, s] for e in range(NE)], axis=0)
        both = jnp.dot(left, right, preferred_element_type=F32)
        value = both[:16] + both[16:]
        out_ref[s] = jnp.where(degree >= order_ref[s], value, 0.0).astype(BF16)


def synthesis(orders, fourier, legendre):
    return pl.pallas_call(
        synthesis_kernel,
        out_shape=jax.ShapeDtypeStruct((SE, 16, DEGREES), BF16),
        in_specs=[
            pl.BlockSpec(memory_space=pltpu.SMEM),
            pl.BlockSpec(memory_space=pltpu.VMEM),
            pl.BlockSpec(memory_space=pltpu.VMEM),
        ],
        out_specs=pl.BlockSpec(memory_space=pltpu.VMEM),
        compiler_params=params(32),
    )(orders, fourier, legendre)


def analysis_kernel(spectral_ref, legendre_ref, out_ref):
    total = sum(spectral_ref[z].astype(F32) for z in range(NZB))
    high, low = split2(total.reshape(NS * 16, DEGREES))
    left = jnp.concatenate([high, low], axis=0)
    both = lax.dot_general(
        left, legendre_ref[...], (((1,), (1,)), ((), ())), preferred_element_type=F32
    )
    value = both[: NS * 16] + both[NS * 16 :]
    own = jnp.concatenate([value[:16, :128], value[16:, 128:]], axis=0)
    flipped = own.T
    out_ref[...] = jnp.concatenate(
        [flipped[g * N_BLK : (g + 1) * N_BLK] for g in range(GB)], axis=1
    )


def analysis(spectral, legendre):
    return pl.pallas_call(
        analysis_kernel,
        out_shape=jax.ShapeDtypeStruct((N_BLK, 128), F32),
        compiler_params=params(32),
    )(spectral, legendre)


def longitude_kernel(value_ref, high_ref, low_ref, out_ref):
    high, low = split2(value_ref[...])

    def product(left, right):
        return lax.dot_general(
            left, right, (((0,), (0,)), ((), ())), preferred_element_type=F32
        )

    table = high_ref[...]
    sums = product(high, table) + (product(high, low_ref[...]) + product(low, table))
    for g in range(GB):
        total = None
        for k in range(2 * NS):
            row = g * 32 + k * 8
            piece = sums[row : row + 8, k * 128 : k * 128 + 128]
            total = piece if total is None else total + piece
        out_ref[:, g, :] = total


def longitude_sums(value, high, low):
    return pl.pallas_call(
        longitude_kernel,
        out_shape=jax.ShapeDtypeStruct((FIELDS, GB, 128), F32),
        compiler_params=params(32),
    )(value, high, low)


def longitude_table(order_slot, order_index):
    pair = order_slot.reshape(ORDERS // NS, NS)
    longitude = order_index * 128 + jnp.arange(128, dtype=jnp.int32)
    product = pair[:, :, None] * longitude[None, None, :] % NLON
    angle = product.astype(F32) * (2.0 * math.pi / NLON)
    scale = 1.0 / math.sqrt(DEGREES)
    table = jnp.stack([jnp.cos(angle) * scale, jnp.sin(angle) * -scale], axis=2)
    return split2(table.reshape(ORDERS // NS, NS * 2 * 128))


def local(cotangent, cycle_slot, order_slot, legendre_healpix, legendre_gauss):
    order_index = lax.axis_index("order")
    blk = lax.axis_index("blk")
    e_index = blk // 8 * NZA + blk % NZA

    columns = order_slot.reshape(N_ORDER * NE, SE).T
    table = pixel_table(columns.reshape(ORDERS))
    own_cycle = lax.dynamic_index_in_dim(cycle_slot, order_index, keepdims=False)
    stride, twice_offset, cycle_scale = cycle_geometry(own_cycle)
    phase = (columns * twice_offset % (2 * NPIX)).astype(F32) * (math.pi / NPIX)
    rc, rs = cycle_scale * jnp.cos(phase), cycle_scale * jnp.sin(phase)
    lon_high, lon_low = longitude_table(order_slot, order_index)
    own_orders = lax.dynamic_slice_in_dim(order_slot, order_index * SLOTS + e_index * SE, SE)

    healpix = exchange(legendre_healpix, "blk", GROUP_E).reshape(NE, SE, RB, DEGREES)
    gauss = exchange(legendre_gauss.reshape(N_BLK, NS * GB, DEGREES), "blk", GROUP_ALL)
    gauss = gauss.transpose(1, 0, 2).reshape(NS * GB * N_BLK, DEGREES)

    pixels = exchange(cotangent.transpose(1, 0, 2), "order")
    fourier = pixel_sums(stride.reshape(1), pixels, table, rc, rs)
    fourier = exchange(fourier.reshape(N_ORDER, NE, 128), "order")
    fourier = exchange(fourier.transpose(1, 0, 2), "blk", GROUP_E)
    spectral = synthesis(own_orders, fourier.reshape(NE * RB, 128), healpix)
    spectral = exchange(spectral.reshape(NZB, NS, 16, DEGREES), "blk", GROUP_Z)
    gaussian = analysis(spectral, gauss)
    gaussian = exchange(gaussian, "blk", GROUP_ALL)
    gathered = exchange(jnp.broadcast_to(gaussian, (N_ORDER, N_BLK, 128)), "order")
    result = longitude_sums(gathered.reshape(N_ORDER * N_BLK, 128), lon_high, lon_low)
    return result.transpose(2, 0, 1)


def solution(mesh):
    placed = (
        P(None, "blk", "order"),
        P("blk"),
        P(),
        P("order", "blk", None),
        P("order", "blk", None),
    )
    return jax.shard_map(
        local, mesh=mesh, in_specs=placed, out_specs=P("order", None, "blk"), check_vma=False
    )
```

```python
import math

import jax
import jax.numpy as jnp
from jax import lax
from jax.experimental import pallas as pl
from jax.experimental.pallas import tpu as pltpu
from jax.sharding import Mesh, PartitionSpec as P

NPIX, NLON, NSIDE = 4096, 2048, 1024
FIELDS, ORDERS, DEGREES = 8, 1024, 1024
N_ORDER, N_BLK = 16, 32
SLOTS = ORDERS // N_ORDER
NE, NH = 4, 8
SE = SLOTS // NE
NS = SE // NH
RB = 16
GB = 4


BLK = ("xb", "xa", "zb", "za")
E_AXES, H_AXES = ("xa", "za"), ("xb", "zb")


def blk_of(e, h):
    return (h // 4 * 2 + e // 2) * 8 + h % 4 * 2 + e % 2


BF16, F32 = jnp.bfloat16, jnp.float32


def own_e():
    return lax.axis_index(E_AXES)


def exchange(value, axes):
    return lax.all_to_all(value, axes, split_axis=0, concat_axis=0, tiled=True)


def split2(value):
    high = value.astype(BF16)
    return high, (value - high.astype(F32)).astype(BF16)


def params(mib):
    return pltpu.CompilerParams(vmem_limit_bytes=mib << 20)


def pixel_kernel(cycle_ref, x_ref, base_ref, columns_ref, out_ref, acc_ref, fine_ref):
    cycle = cycle_ref[lax.axis_index("order")]
    nearest = jnp.minimum(jnp.minimum(cycle, NSIDE), 4 * NSIDE - cycle)
    rounded, stride = 1, NSIDE
    for index in range(NSIDE.bit_length() - 1):
        above = nearest > 2**index
        rounded = jnp.where(above, 2 ** (index + 1), rounded)
        stride = jnp.where(above, NSIDE // 2 ** (index + 1), stride)

    c0, s0 = base_ref[0, 24:32, :], base_ref[1, 24:32, :]
    for b in range(8):
        c1, s1 = base_ref[0, 16 + b : 17 + b, :], base_ref[1, 16 + b : 17 + b, :]
        fine_ref[0, 8 * b : 8 * b + 8, :] = c1 * c0 - s1 * s0
        fine_ref[1, 8 * b : 8 * b + 8, :] = s1 * c0 + c1 * s0
    acc_ref[...] = jnp.zeros_like(acc_ref)

    def step(block, carry):
        column = block * 256 + lax.broadcasted_iota(jnp.int32, (FIELDS, 256), 1)
        keep = (column & (stride - 1)) == 0
        masked = jnp.where(keep, x_ref[block].astype(F32), 0.0).astype(BF16)
        row1 = pl.ds(block // 2, 1)
        coarse = []
        for a in range(4):
            row0 = pl.ds(8 + block % 2 * 4 + a, 1)
            c1, s1 = base_ref[0, row1, :], base_ref[1, row1, :]
            c0, s0 = base_ref[0, row0, :], base_ref[1, row0, :]
            coarse.append((c1 * c0 - s1 * s0, s1 * c0 + c1 * s0))
        for tile in range(ORDERS // 128):
            lanes = slice(tile * 128, tile * 128 + 128)
            cb, sb = fine_ref[0, :, lanes], fine_ref[1, :, lanes]
            cos_rows = [(ca[:, lanes] * cb - sa[:, lanes] * sb).astype(BF16) for ca, sa in coarse]
            sin_rows = [(sa[:, lanes] * cb + ca[:, lanes] * sb).astype(BF16) for ca, sa in coarse]
            table = jnp.concatenate(
                [jnp.concatenate(cos_rows, axis=0), jnp.concatenate(sin_rows, axis=0)], axis=1
            )
            sums = slice(tile * 256, tile * 256 + 256)
            acc_ref[:, sums] += jnp.dot(masked, table, preferred_element_type=F32)
        return carry

    lax.fori_loop(0, N_ORDER, step, 0)
    shifted = (nearest < NSIDE) | (((cycle - NSIDE) & 1) == 0)
    twice = jnp.where(shifted, stride, 0)
    length = jnp.full((1, ORDERS), 4 * rounded, jnp.int32).astype(F32)
    scale = 1.0 / jnp.sqrt(length)
    phase = ((columns_ref[...] * twice) & (2 * NPIX - 1)).astype(F32) * (math.pi / NPIX)
    rc, rs = scale * jnp.cos(phase), scale * jnp.sin(phase)
    real, imag = [], []
    for tile in range(ORDERS // 128):
        lanes = slice(tile * 128, tile * 128 + 128)
        csum = acc_ref[:, tile * 256 : tile * 256 + 128]
        ssum = acc_ref[:, tile * 256 + 128 : tile * 256 + 256]
        real.append(rc[:, lanes] * csum - rs[:, lanes] * ssum)
        imag.append(-(rs[:, lanes] * csum + rc[:, lanes] * ssum))
    pieces = []
    for tiles in (real, imag):
        flipped = jnp.concatenate(tiles, axis=0).T
        pieces += [flipped[:64], flipped[64:]]
    out_ref[...] = jnp.concatenate(pieces, axis=1)


def pixel_sums(cycle_slot, x, columns):
    unit = jnp.asarray([[512], [64], [8], [1]], jnp.int32) * jnp.arange(8, dtype=jnp.int32)
    angle = (unit.reshape(32, 1) * columns % NPIX).astype(F32) * (2.0 * math.pi / NPIX)
    base = jnp.stack([jnp.cos(angle), jnp.sin(angle)])
    return pl.pallas_call(
        pixel_kernel,
        out_shape=jax.ShapeDtypeStruct((64, 256), F32),
        in_specs=[pl.BlockSpec(memory_space=pltpu.SMEM)]
        + [pl.BlockSpec(memory_space=pltpu.VMEM)] * 3,
        out_specs=pl.BlockSpec(memory_space=pltpu.VMEM),
        scratch_shapes=[
            pltpu.VMEM((FIELDS, 2 * ORDERS), F32),
            pltpu.VMEM((2, 64, ORDERS), F32),
        ],
        compiler_params=params(8),
    )(cycle_slot, x, base, columns)


PART = SE * RB + NH * NS * GB


def parts_kernel(healpix_ref, gauss_ref, *out_refs):
    for k, out_ref in enumerate(out_refs):
        e = own_e() ^ k
        rows = pl.multiple_of(e * (SE * RB), SE * RB)
        out_ref[: SE * RB, :] = healpix_ref[pl.ds(rows, SE * RB), :]
        rows = pl.multiple_of(e * (PART - SE * RB), PART - SE * RB)
        out_ref[SE * RB :, :] = gauss_ref[pl.ds(rows, PART - SE * RB), :]


def exchange_parts(healpix, gauss):
    parts = pl.pallas_call(
        parts_kernel,
        out_shape=[jax.ShapeDtypeStruct((PART, DEGREES), BF16)] * NE,
        in_specs=[pl.BlockSpec(memory_space=pltpu.VMEM)] * 2,
        out_specs=[pl.BlockSpec(memory_space=pltpu.VMEM)] * NE,
        compiler_params=params(10),
    )(healpix.reshape(SLOTS * RB, DEGREES), gauss.reshape(SLOTS * GB, DEGREES))
    result = [parts[0]]
    for k in range(1, NE):
        pairs = [(blk_of(e, h), blk_of(e ^ k, h)) for e in range(NE) for h in range(NH)]
        result.append(lax.ppermute(parts[k], BLK, pairs))
    return result


def synthesis_kernel(order_ref, fourier_ref, *refs):
    part_refs, out_ref = refs[:NE], refs[NE]
    own = own_e()
    parts = [fourier_ref[pl.ds(pl.multiple_of((own ^ k) * RB, RB), RB), :] for k in range(NE)]
    flipped = jnp.concatenate(parts, axis=0).T
    degree = lax.broadcasted_iota(jnp.int32, (16, DEGREES), 1)
    for s in range(SE):
        starts = [c * 128 + s % 2 * 64 + s // 2 * 8 for c in range(2)]
        rows = [flipped[start : start + 8] for start in starts]
        left = jnp.concatenate(split2(jnp.concatenate(rows, axis=0)), axis=0)
        right = jnp.concatenate([ref[s * RB : s * RB + RB, :] for ref in part_refs], axis=0)
        both = jnp.dot(left, right, preferred_element_type=F32)
        value = jnp.where(degree >= order_ref[s], both[:16] + both[16:], 0.0)
        out_ref[s // NS, s % NS * 16 : s % NS * 16 + 16, :] = value.astype(BF16)
    for pair in range(NH // 2):
        start = SE * RB + pair * 16
        both = [ref[start : start + 16, :].astype(F32) for ref in part_refs]
        for side in range(2):
            for k in range(0, NE, 2):
                halves = [rows[side * 8 : side * 8 + 8] for rows in both[k : k + 2]]
                value = jnp.concatenate(halves, axis=0).astype(BF16)
                out_ref[pair * 2 + side, 32 + k * 8 : 48 + k * 8, :] = value


def synthesis(orders, fourier, parts):
    return pl.pallas_call(
        synthesis_kernel,
        out_shape=jax.ShapeDtypeStruct((NH, 64, DEGREES), BF16),
        in_specs=[pl.BlockSpec(memory_space=pltpu.SMEM)]
        + [pl.BlockSpec(memory_space=pltpu.VMEM)] * (1 + NE),
        out_specs=pl.BlockSpec(memory_space=pltpu.VMEM),
        compiler_params=params(10),
    )(orders, fourier, *parts)


def analysis_kernel(sums_ref, out_ref):
    total = sum(sums_ref[h, :32, :].astype(F32) for h in range(NH))
    left = jnp.concatenate(split2(total), axis=0)
    legendre = jnp.concatenate([sums_ref[h, 32:, :] for h in range(NH)], axis=0)
    both = lax.dot_general(
        left, legendre, (((1,), (1,)), ((), ())), preferred_element_type=F32
    )
    both = both[:32] + both[32:]
    high, low = split2(both)
    rest = (both - high.astype(F32) - low.astype(F32)).astype(BF16)
    source = lax.broadcasted_iota(jnp.int32, (256, 256), 0)
    block = (own_e() ^ (source >> 3 & 3)) * NH + (source >> 5)
    wanted = (source & 7) * N_BLK + block
    place = wanted == lax.broadcasted_iota(jnp.int32, (256, 256), 1)
    value = jnp.dot(
        jnp.concatenate([high, low, rest], axis=0),
        jnp.where(place, 1.0, 0.0).astype(BF16),
        preferred_element_type=F32,
    )
    value = value[:32] + value[32:64] + value[64:]
    own = jnp.concatenate([value[:16, :128], value[16:, 128:]], axis=0)
    flipped = own.T
    rows = jnp.concatenate([flipped[g * N_BLK : (g + 1) * N_BLK] for g in range(GB)], axis=1)
    for order in range(N_ORDER):
        out_ref[order] = rows


def analysis(sums):
    return pl.pallas_call(
        analysis_kernel,
        out_shape=jax.ShapeDtypeStruct((N_ORDER, N_BLK, 128), F32),
        compiler_params=params(8),
    )(sums)


def longitude_kernel(value_ref, table_ref, out_ref):
    high, low = split2(value_ref[...])
    table, rest = split2(table_ref[...])

    def product(left, right):
        return lax.dot_general(
            left, right, (((0,), (0,)), ((), ())), preferred_element_type=F32
        )

    sums = product(high, table) + (product(high, rest) + product(low, table))
    for g in range(GB):
        total = None
        for k in range(2 * NS):
            row = g * 32 + k * 8
            piece = sums[row : row + 8, k * 128 : k * 128 + 128]
            total = piece if total is None else total + piece
        out_ref[:, g, :] = total


def longitude_sums(value, table):
    return pl.pallas_call(
        longitude_kernel,
        out_shape=jax.ShapeDtypeStruct((FIELDS, GB, 128), F32),
        compiler_params=params(8),
    )(value, table)


def longitude_table(order_slot, order_index):
    pair = order_slot.reshape(ORDERS // NS, NS)
    longitude = order_index * 128 + jnp.arange(128, dtype=jnp.int32)
    product = pair[:, :, None] * longitude[None, None, :] % NLON
    angle = product.astype(F32) * (2.0 * math.pi / NLON)
    scale = 1.0 / math.sqrt(DEGREES)
    table = jnp.stack([jnp.cos(angle) * scale, jnp.sin(angle) * -scale], axis=2)
    return table.reshape(ORDERS // NS, NS * 2 * 128)


def local(cotangent, cycle_slot, order_slot, legendre_healpix, legendre_gauss):
    order_index = lax.axis_index("order")
    columns = order_slot.reshape(N_ORDER, NE, SE).transpose(2, 1, 0).reshape(1, ORDERS)
    lon_table = longitude_table(order_slot, order_index)
    own_orders = lax.dynamic_slice_in_dim(order_slot, order_index * SLOTS + own_e() * SE, SE)

    pixels = exchange(cotangent.transpose(1, 0, 2), "order")
    parts = exchange_parts(legendre_healpix, legendre_gauss)
    fourier = pixel_sums(cycle_slot, pixels, columns)
    fourier = exchange(fourier, E_AXES + ("order",))
    sums = synthesis(own_orders, fourier, parts)
    sums = exchange(sums, H_AXES)
    gaussian = analysis(sums)
    gathered = exchange(gaussian.reshape(N_ORDER * N_BLK, 128), ("order",) + E_AXES + H_AXES)
    result = longitude_sums(gathered, lon_table)
    return result.transpose(2, 0, 1)


def solution(mesh):
    parts = Mesh(mesh.devices.reshape(2, 2, 4, 2, N_ORDER), BLK + ("order",))
    placed = (
        P(None, BLK, "order"),
        P(BLK),
        P(),
        P("order", BLK, None),
        P("order", BLK, None),
    )
    return jax.shard_map(
        local, mesh=parts, in_specs=placed, out_specs=P("order", None, BLK), check_vma=False
    )
```

```python
import math

import jax
import jax.numpy as jnp
from jax import lax
from jax.experimental import pallas as pl
from jax.experimental.pallas import tpu as pltpu
from jax.sharding import Mesh, PartitionSpec as P

NPIX, NLON, NSIDE = 4096, 2048, 1024
FIELDS, ORDERS, DEGREES = 8, 1024, 1024
N_ORDER, N_BLK = 16, 32
SLOTS = ORDERS // N_ORDER
NX, NZ = 4, 8
SE = SLOTS // NX
NS = SE // NZ
RB = 16
GB = 4
BLK = ("x", "z")


BF16, F32 = jnp.bfloat16, jnp.float32


def exchange(value, axes):
    return lax.all_to_all(value, axes, split_axis=0, concat_axis=0, tiled=True)


def split2(value):
    high = value.astype(BF16)
    return high, (value - high.astype(F32)).astype(BF16)


def params(mib):
    return pltpu.CompilerParams(vmem_limit_bytes=mib << 20)


def pixel_kernel(cycle_ref, x_ref, base_ref, columns_ref, out_ref, acc_ref, fine_ref, fold_ref):
    cycle = cycle_ref[lax.axis_index("order")]
    nearest = jnp.minimum(jnp.minimum(cycle, NSIDE), 4 * NSIDE - cycle)
    rounded, stride = 1, NSIDE
    for index in range(NSIDE.bit_length() - 1):
        above = nearest > 2**index
        rounded = jnp.where(above, 2 ** (index + 1), rounded)
        stride = jnp.where(above, NSIDE // 2 ** (index + 1), stride)

    lane = lax.broadcasted_iota(jnp.int32, (FIELDS, 256), 1)
    pixels = []
    for block in range(N_ORDER):
        keep = ((block * 256 + lane) & (stride - 1)) == 0
        pixels.append(jnp.where(keep, x_ref[block].astype(F32), 0.0))
    backward = [15, 14, 13, 12, 7, 6, 5, 4]
    row = lax.broadcasted_iota(jnp.int32, (256, 256), 0)
    col = lax.broadcasted_iota(jnp.int32, (256, 256), 1)
    turn = jnp.where(row + col == 256, 1.0, 0.0).astype(BF16)
    turned = jnp.dot(
        jnp.concatenate([pixels[block] for block in backward], axis=0).astype(BF16),
        turn,
        preferred_element_type=F32,
    )
    for block in range(4):
        first, second = turned[block * 8 : block * 8 + 8], turned[block * 8 + 32 : block * 8 + 40]
        if block:
            first = jnp.where(lane == 0, pixels[16 - block][:, :1], first)
            second = jnp.where(lane == 0, pixels[8 - block][:, :1], second)
        near, far = pixels[block], pixels[8 + block]
        even, odd = near + first, near - first
        other_even, other_odd = second + far, second - far
        cos_rows = split2(even + other_even) + split2(even - other_even)
        sin_rows = split2(odd - other_odd) + split2(odd + other_odd)
        fold_ref[block, 0] = jnp.concatenate(cos_rows, axis=0)
        fold_ref[block, 1] = jnp.concatenate(sin_rows, axis=0)

    c0, s0 = base_ref[0, 18:26, :], base_ref[1, 18:26, :]
    for b in range(8):
        c1, s1 = base_ref[0, 10 + b : 11 + b, :], base_ref[1, 10 + b : 11 + b, :]
        fine_ref[0, 8 * b : 8 * b + 8, :] = c1 * c0 - s1 * s0
        fine_ref[1, 8 * b : 8 * b + 8, :] = s1 * c0 + c1 * s0
    acc_ref[...] = jnp.zeros_like(acc_ref)

    def step(block, carry):
        row1 = pl.ds(block // 2, 1)
        coarse = []
        for a in range(4):
            row0 = pl.ds(2 + block % 2 * 4 + a, 1)
            c1, s1 = base_ref[0, row1, :], base_ref[1, row1, :]
            c0, s0 = base_ref[0, row0, :], base_ref[1, row0, :]
            coarse.append((c1 * c0 - s1 * s0, s1 * c0 + c1 * s0))
        cos_left, sin_left = fold_ref[block, 0], fold_ref[block, 1]
        for tile in range(ORDERS // 256):
            lanes = slice(tile * 256, tile * 256 + 256)
            cb, sb = fine_ref[0, :, lanes], fine_ref[1, :, lanes]
            cos_rows = [(ca[:, lanes] * cb - sa[:, lanes] * sb).astype(BF16) for ca, sa in coarse]
            table = jnp.concatenate(cos_rows, axis=0)
            acc_ref[0, :, lanes] += jnp.dot(cos_left, table, preferred_element_type=F32)
            sin_rows = [(sa[:, lanes] * cb + ca[:, lanes] * sb).astype(BF16) for ca, sa in coarse]
            table = jnp.concatenate(sin_rows, axis=0)
            acc_ref[1, :, lanes] += jnp.dot(sin_left, table, preferred_element_type=F32)
        return carry

    lax.fori_loop(0, 4, step, 0)
    columns = columns_ref[...]
    is_odd = (columns & 1) == 1
    quarter = columns & 3
    cos_quarter = jnp.where(quarter == 0, 1.0, jnp.where(quarter == 2, -1.0, 0.0))
    sin_quarter = jnp.where(quarter == 1, 1.0, jnp.where(quarter == 3, -1.0, 0.0))
    one, three = pixels[4][:, :1], pixels[12][:, :1]
    sums = []
    for part, extra in ((0, (one + three) * cos_quarter), (1, (one - three) * sin_quarter)):
        even = acc_ref[part, 0:8, :] + acc_ref[part, 8:16, :]
        odd = acc_ref[part, 16:24, :] + acc_ref[part, 24:32, :]
        sums.append(jnp.where(is_odd, odd, even) + extra)
    csum, ssum = sums
    shifted = (nearest < NSIDE) | (((cycle - NSIDE) & 1) == 0)
    twice = jnp.where(shifted, stride, 0)
    length = jnp.full((1, ORDERS), 4 * rounded, jnp.int32).astype(F32)
    scale = 1.0 / jnp.sqrt(length)
    phase = ((columns * twice) & (2 * NPIX - 1)).astype(F32) * (math.pi / NPIX)
    rc, rs = scale * jnp.cos(phase), scale * jnp.sin(phase)
    pieces = []
    for value in (rc * csum - rs * ssum, -(rs * csum + rc * ssum)):
        tiles = [value[:, tile * 128 : tile * 128 + 128] for tile in range(8)]
        flipped = jnp.concatenate(tiles, axis=0).T
        pieces += [flipped[:64], flipped[64:]]
    out_ref[...] = jnp.concatenate(pieces, axis=1)


def pixel_sums(cycle_slot, x, columns):
    steps = [512 * a for a in range(2)] + [64 * a for a in range(8)]
    steps = jnp.asarray(steps + [8 * b for b in range(8)] + list(range(8)), jnp.int32)
    angle = (steps[:, None] * columns % NPIX).astype(F32) * (2.0 * math.pi / NPIX)
    base = jnp.stack([jnp.cos(angle), jnp.sin(angle)])
    return pl.pallas_call(
        pixel_kernel,
        out_shape=jax.ShapeDtypeStruct((64, 256), F32),
        in_specs=[pl.BlockSpec(memory_space=pltpu.SMEM)]
        + [pl.BlockSpec(memory_space=pltpu.VMEM)] * 3,
        out_specs=pl.BlockSpec(memory_space=pltpu.VMEM),
        scratch_shapes=[
            pltpu.VMEM((2, 4 * FIELDS, ORDERS), F32),
            pltpu.VMEM((2, 64, ORDERS), F32),
            pltpu.VMEM((4, 2, 4 * FIELDS, 256), BF16),
        ],
        compiler_params=params(8),
    )(cycle_slot, x, base, columns)


def parts_kernel(healpix_ref, *refs):
    out_refs, sems = refs[:NX], refs[NX]
    copies = []
    for k in (1, 2, 3, 0):
        rows = pl.multiple_of((lax.axis_index("x") ^ k) * (SE * RB), SE * RB)
        source = healpix_ref.at[pl.ds(rows, SE * RB), :]
        copies.append(pltpu.make_async_copy(source, out_refs[k], sems.at[k]))
    for copy in copies:
        copy.start()
    for copy in copies:
        copy.wait()


def exchange_parts(healpix):
    parts = pl.pallas_call(
        parts_kernel,
        out_shape=[jax.ShapeDtypeStruct((SE * RB, DEGREES), BF16)] * NX,
        in_specs=[pl.BlockSpec(memory_space=pl.ANY)],
        out_specs=[pl.BlockSpec(memory_space=pltpu.VMEM)] * NX,
        scratch_shapes=[pltpu.SemaphoreType.DMA((NX,))],
        compiler_params=params(10),
    )(healpix.reshape(SLOTS * RB, DEGREES))
    result = [parts[0]]
    for k in range(1, NX):
        result.append(lax.ppermute(parts[k], "x", [(x, x ^ k) for x in range(NX)]))
    return result


def synthesis_kernel(order_ref, fourier_ref, *refs):
    part_refs, out_ref = refs[:NX], refs[NX]
    own = lax.axis_index("x")
    parts = [fourier_ref[pl.ds(pl.multiple_of((own ^ k) * RB, RB), RB), :] for k in range(NX)]
    flipped = jnp.concatenate(parts, axis=0).T
    degree = lax.broadcasted_iota(jnp.int32, (16, DEGREES), 1)
    for s in range(SE):
        starts = [c * 128 + s % 2 * 64 + s // 2 * 8 for c in range(2)]
        rows = [flipped[start : start + 8] for start in starts]
        left = jnp.concatenate(split2(jnp.concatenate(rows, axis=0)), axis=0)
        right = jnp.concatenate([ref[s * RB : s * RB + RB, :] for ref in part_refs], axis=0)
        both = jnp.dot(left, right, preferred_element_type=F32)
        value = jnp.where(degree >= order_ref[s], both[:16] + both[16:], 0.0)
        out_ref[s // NS, s % NS * 16 : s % NS * 16 + 16, :] = value.astype(BF16)


def synthesis(orders, fourier, parts):
    return pl.pallas_call(
        synthesis_kernel,
        out_shape=jax.ShapeDtypeStruct((NZ, NS * 16, DEGREES), BF16),
        in_specs=[pl.BlockSpec(memory_space=pltpu.SMEM)]
        + [pl.BlockSpec(memory_space=pltpu.VMEM)] * (1 + NX),
        out_specs=pl.BlockSpec(memory_space=pltpu.VMEM),
        compiler_params=params(10),
    )(orders, fourier, *parts)


def analysis_kernel(sums_ref, legendre_ref, out_ref):
    total = sum(sums_ref[h].astype(F32) for h in range(NZ))
    left = jnp.concatenate(split2(total), axis=0)
    both = lax.dot_general(
        left, legendre_ref[...], (((1,), (1,)), ((), ())), preferred_element_type=F32
    )
    both = both[:32] + both[32:]
    high, low = split2(both)
    rest = (both - high.astype(F32) - low.astype(F32)).astype(BF16)
    source = lax.broadcasted_iota(jnp.int32, (256, 256), 0)
    wanted = (source & 7) * N_BLK + (source >> 3)
    place = wanted == lax.broadcasted_iota(jnp.int32, (256, 256), 1)
    value = jnp.dot(
        jnp.concatenate([high, low, rest], axis=0),
        jnp.where(place, 1.0, 0.0).astype(BF16),
        preferred_element_type=F32,
    )
    value = value[:32] + value[32:64] + value[64:]
    own = jnp.concatenate([value[:16, :128], value[16:, 128:]], axis=0)
    flipped = own.T
    rows = jnp.concatenate([flipped[g * N_BLK : (g + 1) * N_BLK] for g in range(GB)], axis=1)
    for blk in range(N_BLK):
        out_ref[blk] = jnp.broadcast_to(rows[blk : blk + 1], (N_ORDER, 128))


def analysis(sums, legendre):
    return pl.pallas_call(
        analysis_kernel,
        out_shape=jax.ShapeDtypeStruct((N_BLK, N_ORDER, 128), F32),
        compiler_params=params(8),
    )(sums, legendre)


def longitude_kernel(value_ref, table_ref, out_ref):
    high, low = split2(value_ref[...])
    table, rest = split2(table_ref[...])

    def product(left, right):
        return lax.dot_general(
            left, right, (((0,), (0,)), ((), ())), preferred_element_type=F32
        )

    sums = product(high, table) + (product(high, rest) + product(low, table))
    for g in range(GB):
        total = None
        for k in range(2 * NS):
            row = g * 32 + k * 8
            piece = sums[row : row + 8, k * 128 : k * 128 + 128]
            total = piece if total is None else total + piece
        out_ref[:, g, :] = total


def longitude_sums(value, table):
    return pl.pallas_call(
        longitude_kernel,
        out_shape=jax.ShapeDtypeStruct((FIELDS, GB, 128), F32),
        compiler_params=params(8),
    )(value, table)


def longitude_table(order_slot, order_index):
    pair = order_slot.reshape(N_ORDER, N_BLK, NS).transpose(1, 0, 2)
    pair = pair.reshape(ORDERS // NS, NS)
    longitude = order_index * 128 + jnp.arange(128, dtype=jnp.int32)
    product = pair[:, :, None] * longitude[None, None, :] % NLON
    angle = product.astype(F32) * (2.0 * math.pi / NLON)
    scale = 1.0 / math.sqrt(DEGREES)
    table = jnp.stack([jnp.cos(angle) * scale, jnp.sin(angle) * -scale], axis=2)
    return table.reshape(ORDERS // NS, NS * 2 * 128)


def local(cotangent, cycle_slot, order_slot, legendre_healpix, legendre_gauss):
    order_index = lax.axis_index("order")
    columns = order_slot.reshape(N_ORDER, NX, SE).transpose(2, 1, 0).reshape(1, ORDERS)
    lon_table = longitude_table(order_slot, order_index)
    first_slot = order_index * SLOTS + lax.axis_index("x") * SE
    own_orders = lax.dynamic_slice_in_dim(order_slot, first_slot, SE)

    parts = exchange_parts(legendre_healpix)
    gauss = exchange(legendre_gauss.reshape(N_BLK, NS * GB, DEGREES), BLK)
    gauss, cotangent = lax.optimization_barrier((gauss, cotangent))
    pixels = exchange(cotangent.transpose(1, 0, 2), "order")
    fourier = pixel_sums(cycle_slot, pixels, columns)
    fourier = exchange(fourier, ("x", "order"))
    sums = synthesis(own_orders, fourier, parts)
    sums = exchange(sums, "z")
    gaussian = analysis(sums, gauss.reshape(N_BLK * NS * GB, DEGREES))
    gathered = exchange(gaussian.reshape(N_BLK * N_ORDER, 128), BLK + ("order",))
    result = longitude_sums(gathered, lon_table)
    return result.transpose(2, 0, 1)


def solution(mesh):
    parts = Mesh(mesh.devices.reshape(NX, NZ, N_ORDER), BLK + ("order",))
    placed = (
        P(None, BLK, "order"),
        P(BLK),
        P(),
        P("order", BLK, None),
        P("order", BLK, None),
    )
    return jax.shard_map(
        local, mesh=parts, in_specs=placed, out_specs=P("order", None, BLK), check_vma=False
    )
```

```python
import math

import jax
import jax.numpy as jnp
from jax import lax
from jax.experimental import pallas as pl
from jax.experimental.pallas import tpu as pltpu
from jax.sharding import Mesh, PartitionSpec as P

NPIX, NLON, NSIDE = 4096, 2048, 1024
FIELDS, ORDERS, DEGREES = 8, 1024, 1024
N_ORDER, N_BLK = 16, 32
SLOTS = ORDERS // N_ORDER
NX, NZ = 4, 8
SE = SLOTS // NX
NS = SE // NZ
RB = 16
GB = 4
BLK = ("x", "z")
ORDER = ("ya", "yb")
NA, NB = 4, 4


BF16, F32 = jnp.bfloat16, jnp.float32


def exchange(value, axes):
    return lax.all_to_all(value, axes, split_axis=0, concat_axis=0, tiled=True)


def split2(value):
    high = value.astype(BF16)
    return high, (value - high.astype(F32)).astype(BF16)


def params(mib):
    return pltpu.CompilerParams(vmem_limit_bytes=mib << 20)


def pixel_kernel(
    cycle_ref, x_ref, cos_ref, sin_ref, columns_ref, out_ref, acc_ref, fine_ref, fold_ref
):
    cycle = cycle_ref[lax.axis_index(ORDER)]
    nearest = jnp.minimum(jnp.minimum(cycle, NSIDE), 4 * NSIDE - cycle)
    rounded, stride = 1, NSIDE
    for index in range(NSIDE.bit_length() - 1):
        above = nearest > 2**index
        rounded = jnp.where(above, 2 ** (index + 1), rounded)
        stride = jnp.where(above, NSIDE // 2 ** (index + 1), stride)

    lane = lax.broadcasted_iota(jnp.int32, (FIELDS, 256), 1)
    pixels = []
    for block in range(N_ORDER):
        keep = ((block * 256 + lane) & (stride - 1)) == 0
        pixels.append(jnp.where(keep, x_ref[block].astype(F32), 0.0))
    backward = [15, 14, 13, 12, 7, 6, 5, 4]
    row = lax.broadcasted_iota(jnp.int32, (256, 256), 0)
    col = lax.broadcasted_iota(jnp.int32, (256, 256), 1)
    turn = jnp.where(row + col == 256, 1.0, 0.0).astype(BF16)
    turned = jnp.dot(
        jnp.concatenate([pixels[block] for block in backward], axis=0).astype(BF16),
        turn,
        preferred_element_type=F32,
    )
    for block in range(4):
        first, second = turned[block * 8 : block * 8 + 8], turned[block * 8 + 32 : block * 8 + 40]
        if block:
            first = jnp.where(lane == 0, pixels[16 - block][:, :1], first)
            second = jnp.where(lane == 0, pixels[8 - block][:, :1], second)
        near, far = pixels[block], pixels[8 + block]
        even, odd = near + first, near - first
        other_even, other_odd = second + far, second - far
        cos_rows = split2(even + other_even) + split2(even - other_even)
        sin_rows = split2(odd - other_odd) + split2(odd + other_odd)
        fold_ref[block, 0] = jnp.concatenate(cos_rows, axis=0)
        fold_ref[block, 1] = jnp.concatenate(sin_rows, axis=0)

    c0, s0 = cos_ref[18:26, :], sin_ref[18:26, :]
    for b in range(8):
        c1, s1 = cos_ref[10 + b : 11 + b, :], sin_ref[10 + b : 11 + b, :]
        fine_ref[0, 8 * b : 8 * b + 8, :] = c1 * c0 - s1 * s0
        fine_ref[1, 8 * b : 8 * b + 8, :] = s1 * c0 + c1 * s0
    acc_ref[...] = jnp.zeros_like(acc_ref)

    def step(block, carry):
        row1 = pl.ds(block // 2, 1)
        coarse = []
        for a in range(4):
            row0 = pl.ds(2 + block % 2 * 4 + a, 1)
            c1, s1 = cos_ref[row1, :], sin_ref[row1, :]
            c0, s0 = cos_ref[row0, :], sin_ref[row0, :]
            coarse.append((c1 * c0 - s1 * s0, s1 * c0 + c1 * s0))
        cos_left, sin_left = fold_ref[block, 0], fold_ref[block, 1]
        for tile in range(ORDERS // 256):
            lanes = slice(tile * 256, tile * 256 + 256)
            cb, sb = fine_ref[0, :, lanes], fine_ref[1, :, lanes]
            cos_rows = [(ca[:, lanes] * cb - sa[:, lanes] * sb).astype(BF16) for ca, sa in coarse]
            table = jnp.concatenate(cos_rows, axis=0)
            acc_ref[0, :, lanes] += jnp.dot(cos_left, table, preferred_element_type=F32)
            sin_rows = [(sa[:, lanes] * cb + ca[:, lanes] * sb).astype(BF16) for ca, sa in coarse]
            table = jnp.concatenate(sin_rows, axis=0)
            acc_ref[1, :, lanes] += jnp.dot(sin_left, table, preferred_element_type=F32)
        return carry

    lax.fori_loop(0, 4, step, 0)
    columns = columns_ref[...]
    is_odd = (columns & 1) == 1
    quarter = columns & 3
    cos_quarter = jnp.where(quarter == 0, 1.0, jnp.where(quarter == 2, -1.0, 0.0))
    sin_quarter = jnp.where(quarter == 1, 1.0, jnp.where(quarter == 3, -1.0, 0.0))
    one, three = pixels[4][:, :1], pixels[12][:, :1]
    sums = []
    for part, extra in ((0, (one + three) * cos_quarter), (1, (one - three) * sin_quarter)):
        even = acc_ref[part, 0:8, :] + acc_ref[part, 8:16, :]
        odd = acc_ref[part, 16:24, :] + acc_ref[part, 24:32, :]
        sums.append(jnp.where(is_odd, odd, even) + extra)
    csum, ssum = sums
    shifted = (nearest < NSIDE) | (((cycle - NSIDE) & 1) == 0)
    twice = jnp.where(shifted, stride, 0)
    length = jnp.full((1, ORDERS), 4 * rounded, jnp.int32).astype(F32)
    scale = 1.0 / jnp.sqrt(length)
    phase = ((columns * twice) & (2 * NPIX - 1)).astype(F32) * (math.pi / NPIX)
    rc, rs = scale * jnp.cos(phase), scale * jnp.sin(phase)
    pieces = []
    for value in (rc * csum - rs * ssum, -(rs * csum + rc * ssum)):
        tiles = [value[:, tile * 128 : tile * 128 + 128] for tile in range(8)]
        flipped = jnp.concatenate(tiles, axis=0).T
        pieces += [flipped[:64], flipped[64:]]
    out_ref[...] = jnp.concatenate(pieces, axis=1)


def pixel_sums(cycle_slot, x, columns):
    steps = [512 * a for a in range(2)] + [64 * a for a in range(8)]
    steps = jnp.asarray(steps + [8 * b for b in range(8)] + list(range(8)), jnp.int32)
    angle = (steps[:, None] * columns % NPIX).astype(F32) * (2.0 * math.pi / NPIX)
    return pl.pallas_call(
        pixel_kernel,
        out_shape=jax.ShapeDtypeStruct((64, 256), F32),
        in_specs=[pl.BlockSpec(memory_space=pltpu.SMEM)]
        + [pl.BlockSpec(memory_space=pltpu.VMEM)] * 4,
        out_specs=pl.BlockSpec(memory_space=pltpu.VMEM),
        scratch_shapes=[
            pltpu.VMEM((2, 4 * FIELDS, ORDERS), F32),
            pltpu.VMEM((2, 64, ORDERS), F32),
            pltpu.VMEM((4, 2, 4 * FIELDS, 256), BF16),
        ],
        compiler_params=params(8),
    )(cycle_slot, x, jnp.cos(angle), jnp.sin(angle), columns)


def parts_kernel(healpix_ref, *refs):
    out_refs, sems = refs[:NX], refs[NX]
    copies = []
    for k in (1, 2, 3, 0):
        rows = pl.multiple_of((lax.axis_index("x") ^ k) * (SE * RB), SE * RB)
        source = healpix_ref.at[pl.ds(rows, SE * RB), :]
        copies.append(pltpu.make_async_copy(source, out_refs[k], sems.at[k]))
    for copy in copies:
        copy.start()
    for copy in copies:
        copy.wait()


def exchange_parts(healpix):
    parts = pl.pallas_call(
        parts_kernel,
        out_shape=[jax.ShapeDtypeStruct((SE * RB, DEGREES), BF16)] * NX,
        in_specs=[pl.BlockSpec(memory_space=pl.ANY)],
        out_specs=[pl.BlockSpec(memory_space=pltpu.VMEM)] * NX,
        scratch_shapes=[pltpu.SemaphoreType.DMA((NX,))],
        compiler_params=params(10),
    )(healpix.reshape(SLOTS * RB, DEGREES))
    result = [parts[0]]
    for k in range(1, NX):
        result.append(lax.ppermute(parts[k], "x", [(x, x ^ k) for x in range(NX)]))
    return result


def synthesis_kernel(order_ref, fourier_ref, *refs):
    part_refs, out_ref = refs[:NX], refs[NX]
    own = lax.axis_index("x")
    parts = [fourier_ref[pl.ds(pl.multiple_of((own ^ k) * RB, RB), RB), :] for k in range(NX)]
    flipped = jnp.concatenate(parts, axis=0).T
    degree = lax.broadcasted_iota(jnp.int32, (16, DEGREES), 1)
    for s in range(SE):
        starts = [c * 128 + s % 2 * 64 + s // 2 * 8 for c in range(2)]
        rows = [flipped[start : start + 8] for start in starts]
        left = jnp.concatenate(split2(jnp.concatenate(rows, axis=0)), axis=0)
        right = jnp.concatenate([ref[s * RB : s * RB + RB, :] for ref in part_refs], axis=0)
        both = jnp.dot(left, right, preferred_element_type=F32)
        value = jnp.where(degree >= order_ref[s], both[:16] + both[16:], 0.0)
        out_ref[s // NS, s % NS * 16 : s % NS * 16 + 16, :] = value.astype(BF16)


def synthesis(orders, fourier, parts):
    return pl.pallas_call(
        synthesis_kernel,
        out_shape=jax.ShapeDtypeStruct((NZ, NS * 16, DEGREES), BF16),
        in_specs=[pl.BlockSpec(memory_space=pltpu.SMEM)]
        + [pl.BlockSpec(memory_space=pltpu.VMEM)] * (1 + NX),
        out_specs=pl.BlockSpec(memory_space=pltpu.VMEM),
        compiler_params=params(10),
    )(orders, fourier, *parts)


def analysis_kernel(sums_ref, legendre_ref, out_ref):
    total = sum(sums_ref[h].astype(F32) for h in range(NZ))
    left = jnp.concatenate(split2(total), axis=0)
    both = lax.dot_general(
        left, legendre_ref[...], (((1,), (1,)), ((), ())), preferred_element_type=F32
    )
    both = both[:32] + both[32:]
    high, low = split2(both)
    rest = (both - high.astype(F32) - low.astype(F32)).astype(BF16)
    source = lax.broadcasted_iota(jnp.int32, (256, 256), 0)
    wanted = (source & 7) * N_BLK + (source >> 3)
    place = wanted == lax.broadcasted_iota(jnp.int32, (256, 256), 1)
    value = jnp.dot(
        jnp.concatenate([high, low, rest], axis=0),
        jnp.where(place, 1.0, 0.0).astype(BF16),
        preferred_element_type=F32,
    )
    value = value[:32] + value[32:64] + value[64:]
    own = jnp.concatenate([value[:16, :128], value[16:, 128:]], axis=0)
    flipped = own.T
    rows = jnp.concatenate([flipped[g * N_BLK : (g + 1) * N_BLK] for g in range(GB)], axis=1)
    for blk in range(N_BLK):
        out_ref[blk] = jnp.broadcast_to(rows[blk : blk + 1], (NA, 128))


def analysis(sums, legendre):
    return pl.pallas_call(
        analysis_kernel,
        out_shape=jax.ShapeDtypeStruct((N_BLK, NA, 128), F32),
        compiler_params=params(8),
    )(sums, legendre)


def longitude_kernel(value_ref, *refs):
    high, low = split2(value_ref[...])
    table_refs, out_ref = refs[: 2 * NS], refs[2 * NS]

    def product(left, right):
        return lax.dot_general(
            left, right, (((0,), (0,)), ((), ())), preferred_element_type=F32
        )

    totals = [None] * GB
    for k, table_ref in enumerate(table_refs):
        table, rest = split2(table_ref[...])
        sums = product(high, table) + (product(high, rest) + product(low, table))
        for g in range(GB):
            piece = sums[g * 32 + k * 8 : g * 32 + k * 8 + 8]
            totals[g] = piece if totals[g] is None else totals[g] + piece
    for g in range(GB):
        for b in range(NB):
            out_ref[b, :, g, :] = totals[g][:, b * 128 : b * 128 + 128]


def longitude_sums(value, tables):
    return pl.pallas_call(
        longitude_kernel,
        out_shape=jax.ShapeDtypeStruct((NB, FIELDS, GB, 128), F32),
        compiler_params=params(12),
    )(value, *tables)


def longitude_table(order_slot):
    own_a, own_b = lax.axis_index("ya"), lax.axis_index("yb")
    orders = order_slot.reshape(NA, NB, N_BLK, NS)
    orders = lax.dynamic_index_in_dim(orders, own_b, 1, keepdims=False)
    orders = orders.transpose(1, 0, 2).reshape(N_BLK * NA, NS)
    longitude = own_a * (NB * 128) + jnp.arange(NB * 128, dtype=jnp.int32)
    scale = 1.0 / math.sqrt(DEGREES)
    tables = []
    for s in range(NS):
        product = orders[:, s : s + 1] * longitude[None, :] % NLON
        angle = product.astype(F32) * (2.0 * math.pi / NLON)
        tables += [jnp.cos(angle) * scale, jnp.sin(angle) * -scale]
    return tables


def local(cotangent, cycle_slot, order_slot, legendre_healpix, legendre_gauss):
    order_index = lax.axis_index(ORDER)
    columns = order_slot.reshape(N_ORDER, NX, SE).transpose(2, 1, 0).reshape(1, ORDERS)
    first_slot = order_index * SLOTS + lax.axis_index("x") * SE
    own_orders = lax.dynamic_slice_in_dim(order_slot, first_slot, SE)

    parts = exchange_parts(legendre_healpix)
    gauss = exchange(legendre_gauss, BLK)
    gauss, cotangent, order_slot = lax.optimization_barrier((gauss, cotangent, order_slot))
    pixels = exchange(cotangent.transpose(1, 0, 2), ORDER)
    gauss = gauss.reshape(N_BLK * NS * GB, DEGREES)
    lon_tables = longitude_table(order_slot)
    pixels, gauss, lon_tables, own_orders = lax.optimization_barrier(
        (pixels, gauss, lon_tables, own_orders)
    )
    fourier = pixel_sums(cycle_slot, pixels, columns)
    fourier = exchange(fourier, ("x",) + ORDER)
    sums = synthesis(own_orders, fourier, parts)
    sums = exchange(sums, "z")
    gaussian = analysis(sums, gauss)
    gathered = exchange(gaussian.reshape(N_BLK * NA, 128), BLK + ("ya",))
    result = exchange(longitude_sums(gathered, lon_tables), "yb")
    return jnp.sum(result, axis=0).transpose(2, 0, 1)


def solution(mesh):
    parts = Mesh(mesh.devices.reshape(NX, NZ, NA, NB), BLK + ORDER)
    placed = (
        P(None, BLK, ORDER),
        P(BLK),
        P(),
        P(ORDER, BLK, None),
        P(ORDER, BLK, None),
    )
    return jax.shard_map(
        local, mesh=parts, in_specs=placed, out_specs=P(ORDER, None, BLK), check_vma=False
    )
```

```python
import math

import jax
import jax.numpy as jnp
from jax import lax
from jax.experimental import pallas as pl
from jax.experimental.pallas import tpu as pltpu
from jax.sharding import Mesh, PartitionSpec as P

NPIX, NLON, NSIDE = 4096, 2048, 1024
FIELDS, ORDERS, DEGREES = 8, 1024, 1024
N_ORDER, N_BLK = 16, 32
SLOTS = ORDERS // N_ORDER
NX, NZ = 4, 8
SE = SLOTS // NX
NS = SE // NZ
RB = 16
GB = 4
BLK = ("x", "z")
ORDER = ("ya", "yb")
NA, NB = 4, 4


BF16, F32 = jnp.bfloat16, jnp.float32


def exchange(value, axes):
    return lax.all_to_all(value, axes, split_axis=0, concat_axis=0, tiled=True)


def split2(value):
    high = value.astype(BF16)
    return high, (value - high.astype(F32)).astype(BF16)


def params(mib):
    return pltpu.CompilerParams(vmem_limit_bytes=mib << 20)


def pixel_kernel(
    cycle_ref, x_ref, cos_ref, sin_ref, columns_ref, out_ref, acc_ref, fine_ref, fold_ref
):
    cycle = cycle_ref[lax.axis_index(ORDER)]
    nearest = jnp.minimum(jnp.minimum(cycle, NSIDE), 4 * NSIDE - cycle)
    rounded, stride = 1, NSIDE
    for index in range(NSIDE.bit_length() - 1):
        above = nearest > 2**index
        rounded = jnp.where(above, 2 ** (index + 1), rounded)
        stride = jnp.where(above, NSIDE // 2 ** (index + 1), stride)

    lane = lax.broadcasted_iota(jnp.int32, (FIELDS, 256), 1)
    pixels = []
    for block in range(N_ORDER):
        keep = ((block * 256 + lane) & (stride - 1)) == 0
        pixels.append(jnp.where(keep, x_ref[block].astype(F32), 0.0))
    backward = [15, 14, 13, 12, 7, 6, 5, 4]
    row = lax.broadcasted_iota(jnp.int32, (256, 256), 0)
    col = lax.broadcasted_iota(jnp.int32, (256, 256), 1)
    turn = jnp.where(row + col == 256, 1.0, 0.0).astype(BF16)
    turned = jnp.dot(
        jnp.concatenate([pixels[block] for block in backward], axis=0).astype(BF16),
        turn,
        preferred_element_type=F32,
    )
    for block in range(4):
        first, second = turned[block * 8 : block * 8 + 8], turned[block * 8 + 32 : block * 8 + 40]
        if block:
            first = jnp.where(lane == 0, pixels[16 - block][:, :1], first)
            second = jnp.where(lane == 0, pixels[8 - block][:, :1], second)
        near, far = pixels[block], pixels[8 + block]
        even, odd = near + first, near - first
        other_even, other_odd = second + far, second - far
        cos_rows = split2(even + other_even) + split2(even - other_even)
        sin_rows = split2(odd - other_odd) + split2(odd + other_odd)
        fold_ref[block, 0] = jnp.concatenate(cos_rows, axis=0)
        fold_ref[block, 1] = jnp.concatenate(sin_rows, axis=0)

    c0, s0 = cos_ref[18:26, :], sin_ref[18:26, :]
    for b in range(8):
        c1, s1 = cos_ref[10 + b : 11 + b, :], sin_ref[10 + b : 11 + b, :]
        fine_ref[0, 8 * b : 8 * b + 8, :] = c1 * c0 - s1 * s0
        fine_ref[1, 8 * b : 8 * b + 8, :] = s1 * c0 + c1 * s0
    acc_ref[...] = jnp.zeros_like(acc_ref)

    def step(block, carry):
        row1 = pl.ds(block // 2, 1)
        coarse = []
        for a in range(4):
            row0 = pl.ds(2 + block % 2 * 4 + a, 1)
            c1, s1 = cos_ref[row1, :], sin_ref[row1, :]
            c0, s0 = cos_ref[row0, :], sin_ref[row0, :]
            coarse.append((c1 * c0 - s1 * s0, s1 * c0 + c1 * s0))
        cos_left, sin_left = fold_ref[block, 0], fold_ref[block, 1]
        for tile in range(ORDERS // 256):
            lanes = slice(tile * 256, tile * 256 + 256)
            cb, sb = fine_ref[0, :, lanes], fine_ref[1, :, lanes]
            cos_rows = [(ca[:, lanes] * cb - sa[:, lanes] * sb).astype(BF16) for ca, sa in coarse]
            table = jnp.concatenate(cos_rows, axis=0)
            acc_ref[0, :, lanes] += jnp.dot(cos_left, table, preferred_element_type=F32)
            sin_rows = [(sa[:, lanes] * cb + ca[:, lanes] * sb).astype(BF16) for ca, sa in coarse]
            table = jnp.concatenate(sin_rows, axis=0)
            acc_ref[1, :, lanes] += jnp.dot(sin_left, table, preferred_element_type=F32)
        return carry

    lax.fori_loop(0, 4, step, 0)
    columns = columns_ref[...]
    is_odd = (columns & 1) == 1
    quarter = columns & 3
    cos_quarter = jnp.where(quarter == 0, 1.0, jnp.where(quarter == 2, -1.0, 0.0))
    sin_quarter = jnp.where(quarter == 1, 1.0, jnp.where(quarter == 3, -1.0, 0.0))
    one, three = pixels[4][:, :1], pixels[12][:, :1]
    sums = []
    for part, extra in ((0, (one + three) * cos_quarter), (1, (one - three) * sin_quarter)):
        even = acc_ref[part, 0:8, :] + acc_ref[part, 8:16, :]
        odd = acc_ref[part, 16:24, :] + acc_ref[part, 24:32, :]
        sums.append(jnp.where(is_odd, odd, even) + extra)
    csum, ssum = sums
    shifted = (nearest < NSIDE) | (((cycle - NSIDE) & 1) == 0)
    twice = jnp.where(shifted, stride, 0)
    length = jnp.full((1, ORDERS), 4 * rounded, jnp.int32).astype(F32)
    scale = 1.0 / jnp.sqrt(length)
    phase = ((columns * twice) & (2 * NPIX - 1)).astype(F32) * (math.pi / NPIX)
    rc, rs = scale * jnp.cos(phase), scale * jnp.sin(phase)
    pieces = []
    for value in (rc * csum - rs * ssum, -(rs * csum + rc * ssum)):
        tiles = [value[:, tile * 128 : tile * 128 + 128] for tile in range(8)]
        flipped = jnp.concatenate(tiles, axis=0).T
        pieces += [flipped[:64], flipped[64:]]
    out_ref[...] = jnp.concatenate(pieces, axis=1)


def pixel_sums(cycle_slot, x, columns):
    steps = [512 * a for a in range(2)] + [64 * a for a in range(8)]
    steps = jnp.asarray(steps + [8 * b for b in range(8)] + list(range(8)), jnp.int32)
    angle = (steps[:, None] * columns % NPIX).astype(F32) * (2.0 * math.pi / NPIX)
    return pl.pallas_call(
        pixel_kernel,
        out_shape=jax.ShapeDtypeStruct((64, 256), F32),
        in_specs=[pl.BlockSpec(memory_space=pltpu.SMEM)]
        + [pl.BlockSpec(memory_space=pltpu.VMEM)] * 4,
        out_specs=pl.BlockSpec(memory_space=pltpu.VMEM),
        scratch_shapes=[
            pltpu.VMEM((2, 4 * FIELDS, ORDERS), F32),
            pltpu.VMEM((2, 64, ORDERS), F32),
            pltpu.VMEM((4, 2, 4 * FIELDS, 256), BF16),
        ],
        compiler_params=params(8),
    )(cycle_slot, x, jnp.cos(angle), jnp.sin(angle), columns)


def parts_kernel(healpix_ref, *refs):
    out_refs, sems = refs[:NX], refs[NX]
    copies = []
    for k in (1, 2, 3, 0):
        rows = pl.multiple_of((lax.axis_index("x") ^ k) * (SE * RB), SE * RB)
        source = healpix_ref.at[pl.ds(rows, SE * RB), :]
        copies.append(pltpu.make_async_copy(source, out_refs[k], sems.at[k]))
    for copy in copies:
        copy.start()
    for copy in copies:
        copy.wait()


def exchange_parts(healpix):
    parts = pl.pallas_call(
        parts_kernel,
        out_shape=[jax.ShapeDtypeStruct((SE * RB, DEGREES), BF16)] * NX,
        in_specs=[pl.BlockSpec(memory_space=pl.ANY)],
        out_specs=[pl.BlockSpec(memory_space=pltpu.VMEM)] * NX,
        scratch_shapes=[pltpu.SemaphoreType.DMA((NX,))],
        compiler_params=params(10),
    )(healpix.reshape(SLOTS * RB, DEGREES))
    result = [parts[0]]
    for k in range(1, NX):
        result.append(lax.ppermute(parts[k], "x", [(x, x ^ k) for x in range(NX)]))
    return result


def synthesis_kernel(order_ref, fourier_ref, *refs):
    part_refs, out_ref = refs[:NX], refs[NX]
    own = lax.axis_index("x")
    parts = [fourier_ref[pl.ds(pl.multiple_of((own ^ k) * RB, RB), RB), :] for k in range(NX)]
    flipped = jnp.concatenate(parts, axis=0).T
    degree = lax.broadcasted_iota(jnp.int32, (16, DEGREES), 1)
    for s in range(SE):
        starts = [c * 128 + s % 2 * 64 + s // 2 * 8 for c in range(2)]
        rows = [flipped[start : start + 8] for start in starts]
        left = jnp.concatenate(split2(jnp.concatenate(rows, axis=0)), axis=0)
        right = jnp.concatenate([ref[s * RB : s * RB + RB, :] for ref in part_refs], axis=0)
        both = jnp.dot(left, right, preferred_element_type=F32)
        value = jnp.where(degree >= order_ref[s], both[:16] + both[16:], 0.0)
        out_ref[s // NS, s % NS * 16 : s % NS * 16 + 16, :] = value.astype(BF16)


def synthesis(orders, fourier, parts):
    return pl.pallas_call(
        synthesis_kernel,
        out_shape=jax.ShapeDtypeStruct((NZ, NS * 16, DEGREES), BF16),
        in_specs=[pl.BlockSpec(memory_space=pltpu.SMEM)]
        + [pl.BlockSpec(memory_space=pltpu.VMEM)] * (1 + NX),
        out_specs=pl.BlockSpec(memory_space=pltpu.VMEM),
        compiler_params=params(10),
    )(orders, fourier, *parts)


def analysis_kernel(sums_ref, legendre_ref, out_ref):
    total = sum(sums_ref[h].astype(F32) for h in range(NZ))
    left = jnp.concatenate(split2(total), axis=0)
    both = lax.dot_general(
        left, legendre_ref[...], (((1,), (1,)), ((), ())), preferred_element_type=F32
    )
    both = both[:32] + both[32:]
    high, low = split2(both)
    rest = (both - high.astype(F32) - low.astype(F32)).astype(BF16)
    source = lax.broadcasted_iota(jnp.int32, (256, 256), 0)
    wanted = (source & 7) * N_BLK + (source >> 3)
    place = wanted == lax.broadcasted_iota(jnp.int32, (256, 256), 1)
    value = jnp.dot(
        jnp.concatenate([high, low, rest], axis=0),
        jnp.where(place, 1.0, 0.0).astype(BF16),
        preferred_element_type=F32,
    )
    value = value[:32] + value[32:64] + value[64:]
    own = jnp.concatenate([value[:16, :128], value[16:, 128:]], axis=0)
    flipped = own.T
    rows = jnp.concatenate([flipped[g * N_BLK : (g + 1) * N_BLK] for g in range(GB)], axis=1)
    for a in range(NA):
        out_ref[a] = rows


def analysis(sums, legendre):
    return pl.pallas_call(
        analysis_kernel,
        out_shape=jax.ShapeDtypeStruct((NA, N_BLK, 128), F32),
        compiler_params=params(8),
    )(sums, legendre)


def longitude_kernel(value_ref, *refs):
    high, low = split2(value_ref[...])
    table_refs, out_ref = refs[: 2 * NS], refs[2 * NS]

    def product(left, right):
        return lax.dot_general(
            left, right, (((0,), (0,)), ((), ())), preferred_element_type=F32
        )

    totals = [None] * GB
    for k, table_ref in enumerate(table_refs):
        table, rest = split2(table_ref[...])
        sums = product(high, table) + (product(high, rest) + product(low, table))
        for g in range(GB):
            piece = sums[g * 32 + k * 8 : g * 32 + k * 8 + 8]
            totals[g] = piece if totals[g] is None else totals[g] + piece
    for g in range(GB):
        for b in range(NB):
            out_ref[b, :, g, :] = totals[g][:, b * 128 : b * 128 + 128]


def longitude_sums(value, tables):
    return pl.pallas_call(
        longitude_kernel,
        out_shape=jax.ShapeDtypeStruct((NB, FIELDS, GB, 128), F32),
        compiler_params=params(12),
    )(value, *tables)


def longitude_table(order_slot):
    orders = order_slot.reshape(NA, NB, N_BLK, NS)
    orders = lax.dynamic_index_in_dim(orders, lax.axis_index("ya"), 0, keepdims=False)
    orders = orders.reshape(NB * N_BLK, NS)
    column = jnp.arange(NA * 128, dtype=jnp.int32)
    longitude = (column // 128 * NB + lax.axis_index("yb")) * 128 + column % 128
    scale = 1.0 / math.sqrt(DEGREES)
    tables = []
    for s in range(NS):
        product = orders[:, s : s + 1] * longitude[None, :] % NLON
        angle = product.astype(F32) * (2.0 * math.pi / NLON)
        tables += [jnp.cos(angle) * scale, jnp.sin(angle) * -scale]
    return tables


def local(cotangent, cycle_slot, order_slot, legendre_healpix, legendre_gauss):
    order_index = lax.axis_index(ORDER)
    columns = order_slot.reshape(N_ORDER, NX, SE).transpose(2, 1, 0).reshape(1, ORDERS)
    first_slot = order_index * SLOTS + lax.axis_index("x") * SE
    own_orders = lax.dynamic_slice_in_dim(order_slot, first_slot, SE)

    parts = exchange_parts(legendre_healpix)
    gauss = exchange(legendre_gauss, BLK)
    gauss, cotangent, order_slot = lax.optimization_barrier((gauss, cotangent, order_slot))
    pixels = exchange(cotangent.transpose(1, 0, 2), ORDER)
    gauss = gauss.reshape(N_BLK * NS * GB, DEGREES)
    lon_tables = longitude_table(order_slot)
    pixels, gauss, lon_tables, own_orders = lax.optimization_barrier(
        (pixels, gauss, lon_tables, own_orders)
    )
    fourier = pixel_sums(cycle_slot, pixels, columns)
    fourier = exchange(fourier, ("x",) + ORDER)
    sums = synthesis(own_orders, fourier, parts)
    sums = exchange(sums, "z")
    gaussian = analysis(sums, gauss)
    gathered = exchange(gaussian.reshape(NA * N_BLK, 128), ("yb",) + BLK)
    result = exchange(longitude_sums(gathered, lon_tables), "ya")
    return jnp.sum(result, axis=0).transpose(2, 0, 1)


def solution(mesh):
    parts = Mesh(mesh.devices.reshape(NX, NZ, NA, NB), BLK + ORDER)
    placed = (
        P(None, BLK, ORDER),
        P(BLK),
        P(),
        P(ORDER, BLK, None),
        P(ORDER, BLK, None),
    )
    return jax.shard_map(
        local, mesh=parts, in_specs=placed, out_specs=P(ORDER, None, BLK), check_vma=False
    )
```

```python
import math

import jax
import jax.numpy as jnp
from jax import lax
from jax.experimental import pallas as pl
from jax.experimental.pallas import tpu as pltpu
from jax.sharding import Mesh, PartitionSpec as P

NPIX, NLON, NSIDE = 4096, 2048, 1024
FIELDS, ORDERS, DEGREES = 8, 1024, 1024
N_ORDER, N_BLK = 16, 32
SLOTS = ORDERS // N_ORDER
NX, NZ = 4, 8
SE = SLOTS // NX
NS = SE // NZ
RB = 16
GB = 4
BLK = ("x", "z")
ORDER = ("ya", "yb")
NA, NB = 8, 2


BF16, F32 = jnp.bfloat16, jnp.float32


def exchange(value, axes):
    return lax.all_to_all(value, axes, split_axis=0, concat_axis=0, tiled=True)


def split2(value):
    high = value.astype(BF16)
    return high, (value - high.astype(F32)).astype(BF16)


def params(mib):
    return pltpu.CompilerParams(vmem_limit_bytes=mib << 20)


def pixel_kernel(
    cycle_ref, x_ref, cos_ref, sin_ref, columns_ref, out_ref, acc_ref, fine_ref, fold_ref
):
    cycle = cycle_ref[lax.axis_index(ORDER)]
    nearest = jnp.minimum(jnp.minimum(cycle, NSIDE), 4 * NSIDE - cycle)
    rounded, stride = 1, NSIDE
    for index in range(NSIDE.bit_length() - 1):
        above = nearest > 2**index
        rounded = jnp.where(above, 2 ** (index + 1), rounded)
        stride = jnp.where(above, NSIDE // 2 ** (index + 1), stride)

    lane = lax.broadcasted_iota(jnp.int32, (FIELDS, 256), 1)
    pixels = []
    for block in range(N_ORDER):
        keep = ((block * 256 + lane) & (stride - 1)) == 0
        pixels.append(jnp.where(keep, x_ref[block].astype(F32), 0.0))
    backward = [15, 14, 13, 12, 7, 6, 5, 4]
    row = lax.broadcasted_iota(jnp.int32, (256, 256), 0)
    col = lax.broadcasted_iota(jnp.int32, (256, 256), 1)
    turn = jnp.where(row + col == 256, 1.0, 0.0).astype(BF16)
    turned = jnp.dot(
        jnp.concatenate([pixels[block] for block in backward], axis=0).astype(BF16),
        turn,
        preferred_element_type=F32,
    )
    for block in range(4):
        first, second = turned[block * 8 : block * 8 + 8], turned[block * 8 + 32 : block * 8 + 40]
        if block:
            first = jnp.where(lane == 0, pixels[16 - block][:, :1], first)
            second = jnp.where(lane == 0, pixels[8 - block][:, :1], second)
        near, far = pixels[block], pixels[8 + block]
        even, odd = near + first, near - first
        other_even, other_odd = second + far, second - far
        cos_rows = split2(even + other_even) + split2(even - other_even)
        sin_rows = split2(odd - other_odd) + split2(odd + other_odd)
        fold_ref[block, 0] = jnp.concatenate(cos_rows, axis=0)
        fold_ref[block, 1] = jnp.concatenate(sin_rows, axis=0)

    c0, s0 = cos_ref[18:26, :], sin_ref[18:26, :]
    for b in range(8):
        c1, s1 = cos_ref[10 + b : 11 + b, :], sin_ref[10 + b : 11 + b, :]
        fine_ref[0, 8 * b : 8 * b + 8, :] = c1 * c0 - s1 * s0
        fine_ref[1, 8 * b : 8 * b + 8, :] = s1 * c0 + c1 * s0
    acc_ref[...] = jnp.zeros_like(acc_ref)

    def step(block, carry):
        row1 = pl.ds(block // 2, 1)
        coarse = []
        for a in range(4):
            row0 = pl.ds(2 + block % 2 * 4 + a, 1)
            c1, s1 = cos_ref[row1, :], sin_ref[row1, :]
            c0, s0 = cos_ref[row0, :], sin_ref[row0, :]
            coarse.append((c1 * c0 - s1 * s0, s1 * c0 + c1 * s0))
        cos_left, sin_left = fold_ref[block, 0], fold_ref[block, 1]
        for tile in range(ORDERS // 256):
            lanes = slice(tile * 256, tile * 256 + 256)
            cb, sb = fine_ref[0, :, lanes], fine_ref[1, :, lanes]
            cos_rows = [(ca[:, lanes] * cb - sa[:, lanes] * sb).astype(BF16) for ca, sa in coarse]
            table = jnp.concatenate(cos_rows, axis=0)
            acc_ref[0, :, lanes] += jnp.dot(cos_left, table, preferred_element_type=F32)
            sin_rows = [(sa[:, lanes] * cb + ca[:, lanes] * sb).astype(BF16) for ca, sa in coarse]
            table = jnp.concatenate(sin_rows, axis=0)
            acc_ref[1, :, lanes] += jnp.dot(sin_left, table, preferred_element_type=F32)
        return carry

    lax.fori_loop(0, 4, step, 0)
    columns = columns_ref[...]
    is_odd = (columns & 1) == 1
    quarter = columns & 3
    cos_quarter = jnp.where(quarter == 0, 1.0, jnp.where(quarter == 2, -1.0, 0.0))
    sin_quarter = jnp.where(quarter == 1, 1.0, jnp.where(quarter == 3, -1.0, 0.0))
    one, three = pixels[4][:, :1], pixels[12][:, :1]
    sums = []
    for part, extra in ((0, (one + three) * cos_quarter), (1, (one - three) * sin_quarter)):
        even = acc_ref[part, 0:8, :] + acc_ref[part, 8:16, :]
        odd = acc_ref[part, 16:24, :] + acc_ref[part, 24:32, :]
        sums.append(jnp.where(is_odd, odd, even) + extra)
    csum, ssum = sums
    shifted = (nearest < NSIDE) | (((cycle - NSIDE) & 1) == 0)
    twice = jnp.where(shifted, stride, 0)
    length = jnp.full((1, ORDERS), 4 * rounded, jnp.int32).astype(F32)
    scale = 1.0 / jnp.sqrt(length)
    phase = ((columns * twice) & (2 * NPIX - 1)).astype(F32) * (math.pi / NPIX)
    rc, rs = scale * jnp.cos(phase), scale * jnp.sin(phase)
    pieces = []
    for value in (rc * csum - rs * ssum, -(rs * csum + rc * ssum)):
        tiles = [value[:, tile * 128 : tile * 128 + 128] for tile in range(8)]
        flipped = jnp.concatenate(tiles, axis=0).T
        pieces += [flipped[:64], flipped[64:]]
    out_ref[...] = jnp.concatenate(pieces, axis=1)


def pixel_sums(cycle_slot, x, columns):
    steps = [512 * a for a in range(2)] + [64 * a for a in range(8)]
    steps = jnp.asarray(steps + [8 * b for b in range(8)] + list(range(8)), jnp.int32)
    angle = (steps[:, None] * columns % NPIX).astype(F32) * (2.0 * math.pi / NPIX)
    return pl.pallas_call(
        pixel_kernel,
        out_shape=jax.ShapeDtypeStruct((64, 256), F32),
        in_specs=[pl.BlockSpec(memory_space=pltpu.SMEM)]
        + [pl.BlockSpec(memory_space=pltpu.VMEM)] * 4,
        out_specs=pl.BlockSpec(memory_space=pltpu.VMEM),
        scratch_shapes=[
            pltpu.VMEM((2, 4 * FIELDS, ORDERS), F32),
            pltpu.VMEM((2, 64, ORDERS), F32),
            pltpu.VMEM((4, 2, 4 * FIELDS, 256), BF16),
        ],
        compiler_params=params(8),
    )(cycle_slot, x, jnp.cos(angle), jnp.sin(angle), columns)


def parts_kernel(healpix_ref, *refs):
    out_refs, sems = refs[:NX], refs[NX]
    copies = []
    for k in (1, 2, 3, 0):
        rows = pl.multiple_of((lax.axis_index("x") ^ k) * (SE * RB), SE * RB)
        source = healpix_ref.at[pl.ds(rows, SE * RB), :]
        copies.append(pltpu.make_async_copy(source, out_refs[k], sems.at[k]))
    for copy in copies:
        copy.start()
    for copy in copies:
        copy.wait()


def exchange_parts(healpix):
    parts = pl.pallas_call(
        parts_kernel,
        out_shape=[jax.ShapeDtypeStruct((SE * RB, DEGREES), BF16)] * NX,
        in_specs=[pl.BlockSpec(memory_space=pl.ANY)],
        out_specs=[pl.BlockSpec(memory_space=pltpu.VMEM)] * NX,
        scratch_shapes=[pltpu.SemaphoreType.DMA((NX,))],
        compiler_params=params(10),
    )(healpix.reshape(SLOTS * RB, DEGREES))
    result = [parts[0]]
    for k in range(1, NX):
        result.append(lax.ppermute(parts[k], "x", [(x, x ^ k) for x in range(NX)]))
    return result


def synthesis_kernel(order_ref, fourier_ref, *refs):
    part_refs, out_ref = refs[:NX], refs[NX]
    own = lax.axis_index("x")
    parts = [fourier_ref[pl.ds(pl.multiple_of((own ^ k) * RB, RB), RB), :] for k in range(NX)]
    flipped = jnp.concatenate(parts, axis=0).T
    degree = lax.broadcasted_iota(jnp.int32, (16, DEGREES), 1)
    for s in range(SE):
        starts = [c * 128 + s % 2 * 64 + s // 2 * 8 for c in range(2)]
        rows = [flipped[start : start + 8] for start in starts]
        left = jnp.concatenate(split2(jnp.concatenate(rows, axis=0)), axis=0)
        right = jnp.concatenate([ref[s * RB : s * RB + RB, :] for ref in part_refs], axis=0)
        both = jnp.dot(left, right, preferred_element_type=F32)
        value = jnp.where(degree >= order_ref[s], both[:16] + both[16:], 0.0)
        out_ref[s // NS, s % NS * 16 : s % NS * 16 + 16, :] = value.astype(BF16)


def synthesis(orders, fourier, parts):
    return pl.pallas_call(
        synthesis_kernel,
        out_shape=jax.ShapeDtypeStruct((NZ, NS * 16, DEGREES), BF16),
        in_specs=[pl.BlockSpec(memory_space=pltpu.SMEM)]
        + [pl.BlockSpec(memory_space=pltpu.VMEM)] * (1 + NX),
        out_specs=pl.BlockSpec(memory_space=pltpu.VMEM),
        compiler_params=params(10),
    )(orders, fourier, *parts)


def analysis_kernel(sums_ref, legendre_ref, out_ref):
    total = sum(sums_ref[h].astype(F32) for h in range(NZ))
    left = jnp.concatenate(split2(total), axis=0)
    both = lax.dot_general(
        left, legendre_ref[...], (((1,), (1,)), ((), ())), preferred_element_type=F32
    )
    both = both[:32] + both[32:]
    high, low = split2(both)
    rest = (both - high.astype(F32) - low.astype(F32)).astype(BF16)
    source = lax.broadcasted_iota(jnp.int32, (256, 256), 0)
    wanted = (source & 7) * N_BLK + (source >> 3)
    place = wanted == lax.broadcasted_iota(jnp.int32, (256, 256), 1)
    value = jnp.dot(
        jnp.concatenate([high, low, rest], axis=0),
        jnp.where(place, 1.0, 0.0).astype(BF16),
        preferred_element_type=F32,
    )
    value = value[:32] + value[32:64] + value[64:]
    own = jnp.concatenate([value[:16, :128], value[16:, 128:]], axis=0)
    flipped = own.T
    rows = jnp.concatenate([flipped[g * N_BLK : (g + 1) * N_BLK] for g in range(GB)], axis=1)
    for b in range(NB):
        out_ref[b] = rows


def analysis(sums, legendre):
    return pl.pallas_call(
        analysis_kernel,
        out_shape=jax.ShapeDtypeStruct((NB, N_BLK, 128), F32),
        compiler_params=params(8),
    )(sums, legendre)


def longitude_kernel(value_ref, *refs):
    high, low = split2(value_ref[...])
    table_refs, out_ref = refs[: 2 * NS], refs[2 * NS]

    def product(left, right):
        return lax.dot_general(
            left, right, (((0,), (0,)), ((), ())), preferred_element_type=F32
        )

    totals = [None] * GB
    for k, table_ref in enumerate(table_refs):
        table, rest = split2(table_ref[...])
        sums = product(high, table) + (product(high, rest) + product(low, table))
        for g in range(GB):
            piece = sums[g * 32 + k * 8 : g * 32 + k * 8 + 8]
            totals[g] = piece if totals[g] is None else totals[g] + piece
    for g in range(GB):
        for a in range(NA):
            out_ref[a, :, g, :] = totals[g][:, a * 128 : a * 128 + 128]


def longitude_sums(value, tables):
    return pl.pallas_call(
        longitude_kernel,
        out_shape=jax.ShapeDtypeStruct((NA, FIELDS, GB, 128), F32),
        compiler_params=params(12),
    )(value, *tables)


def longitude_table(order_slot):
    orders = order_slot.reshape(NA, NB, N_BLK, NS)
    orders = lax.dynamic_index_in_dim(orders, lax.axis_index("ya"), 0, keepdims=False)
    orders = orders.reshape(NB * N_BLK, NS)
    column = jnp.arange(NA * 128, dtype=jnp.int32)
    longitude = (column // 128 * NB + lax.axis_index("yb")) * 128 + column % 128
    scale = 1.0 / math.sqrt(DEGREES)
    tables = []
    for s in range(NS):
        product = orders[:, s : s + 1] * longitude[None, :] % NLON
        angle = product.astype(F32) * (2.0 * math.pi / NLON)
        tables += [jnp.cos(angle) * scale, jnp.sin(angle) * -scale]
    return tables


def local(cotangent, cycle_slot, order_slot, legendre_healpix, legendre_gauss):
    order_index = lax.axis_index(ORDER)
    columns = order_slot.reshape(N_ORDER, NX, SE).transpose(2, 1, 0).reshape(1, ORDERS)
    first_slot = order_index * SLOTS + lax.axis_index("x") * SE
    own_orders = lax.dynamic_slice_in_dim(order_slot, first_slot, SE)

    parts = exchange_parts(legendre_healpix)
    gauss = exchange(legendre_gauss, BLK)
    gauss, cotangent, order_slot = lax.optimization_barrier((gauss, cotangent, order_slot))
    pixels = exchange(cotangent.transpose(1, 0, 2), ORDER)
    gauss = gauss.reshape(N_BLK * NS * GB, DEGREES)
    lon_tables = longitude_table(order_slot)
    pixels, gauss, lon_tables, own_orders = lax.optimization_barrier(
        (pixels, gauss, lon_tables, own_orders)
    )
    fourier = pixel_sums(cycle_slot, pixels, columns)
    fourier = exchange(fourier, ("x",) + ORDER)
    sums = synthesis(own_orders, fourier, parts)
    sums = exchange(sums, "z")
    gaussian = analysis(sums, gauss)
    gathered = exchange(gaussian.reshape(NB * N_BLK, 128), ("yb",) + BLK)
    result = exchange(longitude_sums(gathered, lon_tables), "ya")
    return jnp.sum(result, axis=0).transpose(2, 0, 1)


def solution(mesh):
    parts = Mesh(mesh.devices.reshape(NX, NZ, NA, NB), BLK + ORDER)
    placed = (
        P(None, BLK, ORDER),
        P(BLK),
        P(),
        P(ORDER, BLK, None),
        P(ORDER, BLK, None),
    )
    return jax.shard_map(
        local, mesh=parts, in_specs=placed, out_specs=P(ORDER, None, BLK), check_vma=False
    )
```
